32 devices in a mesh: ctx: 16 (over z, y, x), head: 2 (over core).
Axes of the slice: x: 2, y: 2, z: 4, core: 2. Of those that a mesh axis runs over, the one named last changes fastest.
Arguments:
- queries: bfloat16 [4096, 4, 256], P('ctx', 'head'), may hold values from -6 to 6
- token_keys: bfloat16 [4096, 4, 256], P('ctx', 'head'), may hold values from -6 to 6
- token_values: bfloat16 [4096, 4, 256], P('ctx', 'head'), may hold values from -6 to 6
- step_rates: float32 [4096, 4], P('ctx', 'head'), may hold values from 0.1 to 1
- counts: int32 [16], replicated, may hold values from 64 to 256, as said below
- fast_weights: float32 [4, 3, 256, 256], P('head'), may hold values from -0.375 to 0.375
- out_weight: bfloat16 [1024, 4096], P('head'), may hold values from -0.1875 to 0.1875
Outputs:
- layer_output: bfloat16 [4096, 4096], P('ctx', 'head')
The draws below stay inside these ranges and needn't reach their ends.
Inputs may be any that keep to these rules, and one draw needn't show every extreme that they name: counts[i] tokens at the start of block i are valid, the rest are padding; some block is full and some holds exactly 64.
All inputs are finite; a program needn't handle non-finite values.
Results may differ from the reference program's by a relative error of at most 0.012.
The reference program's roundings to bfloat16 on the way count: a program that leaves them out, or rounds other values in their place, can miss the bound.
Values may be sent and summed in bfloat16 or wider, within the bound.
A program may use at most 64 MiB of HBM per device.

```python
import math
import jax
import jax.numpy as jnp
from jax import lax

HS = 256
DM = 4096
TOK_DEV = 256
WINDOW = 512
HEADS = 4
BLOCKS = 16
TOKENS = 4096


def draw_queries(key, part):
    result = jnp.clip(1.4 * jax.random.normal(jax.random.fold_in(key, 1), (TOKENS, HEADS, HS), jnp.float32), -6.0, 6.0)
    return result.astype(jnp.bfloat16)


def draw_token_keys(key, part):
    result = jnp.clip(1.4 * jax.random.normal(jax.random.fold_in(key, 2), (TOKENS, HEADS, HS), jnp.float32), -6.0, 6.0)
    return result.astype(jnp.bfloat16)


def draw_counts(key, part):
    drawn = jax.random.randint(jax.random.fold_in(key, 3), (BLOCKS,), TOK_DEV // 4, TOK_DEV + 1)
    fullest = jax.random.randint(jax.random.fold_in(key, 5), (), 0, BLOCKS)
    offset = jax.random.randint(jax.random.fold_in(key, 9), (), 1, BLOCKS)
    smallest = (fullest + offset) % BLOCKS
    drawn = drawn.at[fullest].set(TOK_DEV)
    drawn = drawn.at[smallest].set(TOK_DEV // 4)
    return drawn.astype(jnp.int32)


def shard_levels(own_key, dims, shards, low, high):
    loudness, own = 1.0, jax.random.fold_in(own_key, 6)
    for dim, parts in shards:
        draws = jnp.exp(jax.random.uniform(jax.random.fold_in(own, dim), (parts,), jnp.float32, low / len(shards), high / len(shards)))
        loudness = loudness * jnp.repeat(draws, dims[dim] // parts).reshape([-1 if axis == dim else 1 for axis in range(len(dims))])
    return loudness


def normal_values(rng, dims, spread, bound, split=(), kind=jnp.bfloat16):
    values = jax.random.normal(rng, dims, jnp.float32) * spread
    if len(split) > 0:
        values = shard_levels(rng, dims, split, -0.22, 0.18) * values
    return jnp.clip(values, min=-bound, max=bound).astype(kind)


def setup_inputs(seed: int = 0) -> dict:
    streams_of = jax.random.split(jax.random.key(seed), 8)
    queries = draw_queries(jax.random.fold_in(streams_of[7], 71), 0)
    token_keys = draw_token_keys(jax.random.fold_in(streams_of[7], 71), 0)
    token_values = normal_values(streams_of[2], (TOKENS, HEADS, HS), 1.0, 6.0, ((0, 16), (1, 2)))
    step_rates = jnp.clip(jnp.exp(math.log(1.0) - 2.3025851 * jax.random.uniform(streams_of[3], (TOKENS, HEADS), jnp.float32) ** shard_levels(streams_of[3], (TOKENS, HEADS), ((0, 16), (1, 2)), -0.2, 0.2)), 0.1, 1.0)
    counts = draw_counts(jax.random.fold_in(streams_of[7], 71), 0)
    fast_weights = normal_values(streams_of[5], (HEADS, 3, HS, HS), HS ** -0.5, 0.375, ((0, 2),), jnp.float32)
    out_weight = normal_values(streams_of[6], (HEADS * HS, DM), (HEADS * HS) ** -0.5, 0.1875, ((0, 2),))
    return {"queries": queries, "token_keys": token_keys, "token_values": token_values, "step_rates": step_rates, "counts": counts, "fast_weights": fast_weights, "out_weight": out_weight}


def rounded(values_in):
    return lax.optimization_barrier(values_in.astype(jnp.bfloat16)).astype(jnp.float32)

def silu_slope(pre_value):
    sigmoid_value = jax.nn.sigmoid(pre_value)
    return sigmoid_value * (1.0 + pre_value * (1.0 - sigmoid_value))

def block_gradient(key_block, scaled_block, weights_wide):
    keys_wide = key_block.astype(jnp.float32)
    gate_pre = jnp.einsum('thi,hci->thc', keys_wide, weights_wide[:, 0])
    up_pre = jnp.einsum('thi,hci->thc', keys_wide, weights_wide[:, 1])
    gate_act = jax.nn.silu(gate_pre)
    hidden = rounded(gate_act * up_pre)
    grad_down = -jnp.einsum('thd,thc->hdc', scaled_block, hidden)
    back_hidden = -jnp.einsum('thd,hdc->thc', scaled_block, weights_wide[:, 2])
    grad_gate = rounded(back_hidden * up_pre * silu_slope(gate_pre))
    grad_up = rounded(back_hidden * gate_act)
    first_grad = jnp.einsum('thc,thi->hci', grad_gate, keys_wide)
    second_grad = jnp.einsum('thc,thi->hci', grad_up, keys_wide)
    return jnp.stack([first_grad, second_grad, grad_down], axis=1)

def reference(queries, token_keys, token_values, step_rates, counts, fast_weights, out_weight):
    positions = jnp.arange(TOKENS, dtype=jnp.int32)
    valid_rows = (positions % TOK_DEV < counts[positions // TOK_DEV]).astype(jnp.float32)
    weights_wide = rounded(fast_weights)

    def add_block(total, block_index):
        start = (block_index * TOK_DEV).astype(jnp.int32)
        key_block = lax.dynamic_slice_in_dim(token_keys, start, TOK_DEV, 0)
        value_block = lax.dynamic_slice_in_dim(token_values, start, TOK_DEV, 0).astype(jnp.float32)
        rate_block = lax.dynamic_slice_in_dim(step_rates, start, TOK_DEV, 0)
        valid_block = lax.dynamic_slice_in_dim(valid_rows, start, TOK_DEV, 0)
        scaled_block = rounded((rate_block * valid_block[:, None])[:, :, None] * value_block)
        return (total + block_gradient(key_block, scaled_block, weights_wide), None)
    gradient, _ = lax.scan(add_block, jnp.zeros((HEADS, 3, HS, HS), jnp.float32), jnp.arange(BLOCKS, dtype=jnp.int32))
    updated = fast_weights - gradient / math.sqrt(TOKENS)
    old_norm = jnp.sqrt(lax.optimization_barrier(jnp.sum(fast_weights * fast_weights, axis=-1, keepdims=True)))
    new_weights = rounded(updated * old_norm / jnp.sqrt(lax.optimization_barrier(jnp.sum(updated * updated, axis=-1, keepdims=True)) + 1e-06))
    pad_keys = jnp.concatenate([jnp.zeros((WINDOW, HEADS, HS), jnp.bfloat16), token_keys], 0)
    pad_values = jnp.concatenate([jnp.zeros((WINDOW, HEADS, HS), jnp.bfloat16), token_values], 0)
    pad_valid = jnp.concatenate([jnp.zeros((WINDOW,), jnp.float32), valid_rows], 0)
    distance = WINDOW + jnp.arange(TOK_DEV, dtype=jnp.int32)[:, None] - jnp.arange(WINDOW + TOK_DEV, dtype=jnp.int32)[None, :]

    def one_block(block_index):
        start = (block_index * TOK_DEV).astype(jnp.int32)
        query_block = lax.dynamic_slice_in_dim(queries, start, TOK_DEV, 0).astype(jnp.float32)
        query_valid = lax.dynamic_slice_in_dim(valid_rows, start, TOK_DEV, 0)
        seen_keys = lax.dynamic_slice_in_dim(pad_keys, start, WINDOW + TOK_DEV, 0).astype(jnp.float32)
        seen_values = lax.dynamic_slice_in_dim(pad_values, start, WINDOW + TOK_DEV, 0).astype(jnp.float32)
        seen_valid = lax.dynamic_slice_in_dim(pad_valid, start, WINDOW + TOK_DEV, 0)
        query_gate = jnp.einsum('thi,hci->thc', query_block, new_weights[:, 0])
        query_up = jnp.einsum('thi,hci->thc', query_block, new_weights[:, 1])
        query_hidden = rounded(jax.nn.silu(query_gate) * query_up)
        ttt_out = jnp.einsum('thc,hdc->thd', query_hidden, new_weights[:, 2])
        scores = jnp.einsum('thi,shi->hts', query_block, seen_keys) / math.sqrt(HS)
        allowed = (distance >= 0) & (distance < WINDOW) & (seen_valid[None, :] > 0.5)
        scores = jnp.where(allowed[None], scores, -1e+30)
        top_score = lax.optimization_barrier(jnp.max(scores, axis=-1, keepdims=True))
        expo = jnp.exp(scores - top_score)
        attention = rounded(expo / lax.optimization_barrier(jnp.sum(expo, axis=-1, keepdims=True)))
        window_out = jnp.einsum('hts,shd->thd', attention, seen_values)
        features = ((ttt_out + window_out) * query_valid[:, None, None]).astype(jnp.bfloat16)
        features = features.reshape(TOK_DEV, HEADS * HS)
        return jnp.dot(features, out_weight, preferred_element_type=jnp.float32).astype(jnp.bfloat16)
    outputs = lax.map(one_block, jnp.arange(BLOCKS, dtype=jnp.int32))
    return outputs.reshape(TOKENS, DM)
```

```python
import functools
import math

import jax
import jax.numpy as jnp
from jax import lax
from jax.experimental import pallas as pl
from jax.experimental.pallas import tpu as pltpu
from jax.sharding import PartitionSpec as P

SPAN = 2
NT = (((1,), (1,)), ((), ()))
NN = (((1,), (0,)), ((), ()))
TN = (((0,), (0,)), ((), ()))


def dot(a, b, dims):
    return lax.dot_general(a, b, dims, preferred_element_type=jnp.float32)


def passed_along(value, axis, steps):
    count = lax.axis_size(axis)
    leading, last = (max(0, -steps), min(count, count - steps))
    return lax.ppermute(value, axis, [(source, source + steps) for source in range(leading, last)])


def silu_slope(pre_value):
    sigmoid_value = jax.nn.sigmoid(pre_value)
    return sigmoid_value * (1.0 + pre_value * (1.0 - sigmoid_value))


def refresh(old_rows, gradient_rows, token_total):
    updated = old_rows - gradient_rows / math.sqrt(token_total)
    old_norm = jnp.sqrt(jnp.sum(old_rows * old_rows, axis=-1, keepdims=True))
    fresh = (
        updated * old_norm / jnp.sqrt(jnp.sum(updated * updated, axis=-1, keepdims=True) + 1e-06)
    )
    return fresh.astype(jnp.bfloat16)


def plain_shards(queries, token_keys, token_values, step_rates, counts, fast_weights, out_weight):
    tok_rows, head_local, head_width = queries.shape
    device_count = lax.axis_size("ctx")
    device_place = lax.axis_index("ctx")
    positions = jnp.arange(tok_rows, dtype=jnp.int32)
    own_count = lax.dynamic_index_in_dim(counts, device_place, 0, keepdims=False)
    valid_rows = (positions < own_count).astype(jnp.float32)
    weights_low = fast_weights.astype(jnp.bfloat16)
    gate_pre = jnp.einsum(
        "thi,hci->thc", token_keys, weights_low[:, 0], preferred_element_type=jnp.float32
    )
    up_pre = jnp.einsum(
        "thi,hci->thc", token_keys, weights_low[:, 1], preferred_element_type=jnp.float32
    )
    gate_act = jax.nn.silu(gate_pre)
    hidden = (gate_act * up_pre).astype(jnp.bfloat16)
    scaled = (
        (step_rates * valid_rows[:, None])[:, :, None] * token_values.astype(jnp.float32)
    ).astype(jnp.bfloat16)
    grad_down = -jnp.einsum("thd,thc->hdc", scaled, hidden, preferred_element_type=jnp.float32)
    back_hidden = -jnp.einsum(
        "thd,hdc->thc", scaled, weights_low[:, 2], preferred_element_type=jnp.float32
    )
    grad_gate = (back_hidden * up_pre * silu_slope(gate_pre)).astype(jnp.bfloat16)
    grad_up = (back_hidden * gate_act).astype(jnp.bfloat16)
    first_grad = jnp.einsum(
        "thc,thi->hci", grad_gate, token_keys, preferred_element_type=jnp.float32
    )
    second_grad = jnp.einsum(
        "thc,thi->hci", grad_up, token_keys, preferred_element_type=jnp.float32
    )
    local_grad = jnp.stack([first_grad, second_grad, grad_down], axis=1).reshape(-1, head_width)
    old_flat = fast_weights.reshape(-1, head_width)
    token_total = tok_rows * device_count
    grad_whole = lax.psum(local_grad, "ctx")
    new_flat = refresh(old_flat, grad_whole, token_total)
    new_weights = new_flat.reshape(head_local, 3, head_width, head_width)
    query_gate = jnp.einsum(
        "thi,hci->thc", queries, new_weights[:, 0], preferred_element_type=jnp.float32
    )
    query_up = jnp.einsum(
        "thi,hci->thc", queries, new_weights[:, 1], preferred_element_type=jnp.float32
    )
    query_hidden = (jax.nn.silu(query_gate) * query_up).astype(jnp.bfloat16)
    ttt_out = jnp.einsum(
        "thc,hdc->thd", query_hidden, new_weights[:, 2], preferred_element_type=jnp.float32
    )
    key_parts = []
    value_parts = []
    valid_parts = []
    for back_step in range(SPAN, 0, -1):
        moved_keys, moved_values = passed_along((token_keys, token_values), "ctx", back_step)
        source = device_place - back_step
        source_count = lax.dynamic_index_in_dim(counts, jnp.maximum(source, 0), 0, keepdims=False)
        valid_parts.append(((positions < source_count) & (source >= 0)).astype(jnp.float32))
        key_parts.append(moved_keys)
        value_parts.append(moved_values)
    key_parts.append(token_keys)
    value_parts.append(token_values)
    valid_parts.append(valid_rows)
    seen_keys = jnp.concatenate(key_parts, 0)
    seen_values = jnp.concatenate(value_parts, 0)
    seen_valid = jnp.concatenate(valid_parts, 0)
    window_len = SPAN * tok_rows
    distance = (
        window_len
        + positions[:, None]
        - jnp.arange(window_len + tok_rows, dtype=jnp.int32)[None, :]
    )
    scores = jnp.einsum(
        "thi,shi->hts", queries, seen_keys, preferred_element_type=jnp.float32
    ) / math.sqrt(head_width)
    allowed = (distance >= 0) & (distance < window_len) & (seen_valid[None, :] > 0.5)
    scores = jnp.where(allowed[None], scores, -1e30)
    top_score = jnp.max(scores, axis=-1, keepdims=True)
    expo = jnp.exp(scores - top_score)
    attention = (expo / jnp.sum(expo, axis=-1, keepdims=True)).astype(jnp.bfloat16)
    window_out = jnp.einsum(
        "hts,shd->thd", attention, seen_values, preferred_element_type=jnp.float32
    )
    features = ((ttt_out + window_out) * valid_rows[:, None, None]).astype(jnp.bfloat16)
    features = features.reshape(tok_rows, head_local * head_width)
    partial_out = jnp.dot(features, out_weight, preferred_element_type=jnp.float32)
    return lax.psum_scatter(
        partial_out.astype(jnp.bfloat16), "head", scatter_dimension=1, tiled=True
    )


def kernel(
    n, plane, counts, q, k, v, rates, fw, ow, out,
    grads, part_in, part, last_in, fresh, halo_k, halo_v, window, wide, feats,
    p1_s, p1_r, p2_s, p2_r, g1_s, g1_r, g2_s, g2_r, far_s, far_r, near_s, near_r,
    w_s, w_r, w_l, f_s, f_r,
):
    tok, width = q.shape
    hs = fw.shape[-1]
    heads = width // hs
    depth = n // plane
    wide_rows, rows = hs // plane, hs // n
    cols = out.shape[1]
    c, side = lax.axis_index("ctx"), lax.axis_index("head")
    place, layer = lax.rem(c, plane), lax.div(c, plane)
    even = lax.rem(c, 2) == 0

    def in_plane(d):
        return layer * plane + lax.rem(place + d, plane)

    def in_line(d):
        return lax.rem(layer + d, depth) * plane + place

    def remote(src, dst, send, recv, **device):
        return pltpu.make_async_remote_copy(
            src, dst, send, recv, device_id=device, device_id_type=pl.DeviceIdType.MESH
        )

    barrier = pltpu.get_barrier_semaphore()

    def greet(**device):
        pl.semaphore_signal(
            barrier, inc=1, device_id=device, device_id_type=pl.DeviceIdType.MESH
        )

    for d in range(1, plane):
        greet(ctx=in_plane(d))
    for d in range(1, depth):
        greet(ctx=in_line(d))
    greet(head=1 - side)

    @pl.when(c >= 2)
    def _():
        greet(ctx=c - 2)

    @pl.when(jnp.logical_not(even))
    def _():
        greet(ctx=c - 1)

    @pl.when(even & (c >= 2))
    def _():
        greet(ctx=c + 1)

    sends = (
        plane + depth - 1
        + jnp.where(c + 2 < n, 1, 0)
        + jnp.where(even | (c >= 2), 1, 0)
    )
    pl.semaphore_wait(barrier, sends)

    def far(i):
        src, dst = ((k, halo_k), (v, halo_v))[i]
        return remote(src, dst.at[0], far_s.at[i], far_r.at[i], ctx=c + 2)

    def near(i):
        src, dst = ((k, halo_k), (v, halo_v))[i]
        return remote(src, dst.at[1], near_s.at[i], near_r.at[i], ctx=c + 1)

    def forward(i):
        buf = (halo_k, halo_v)[i]
        return remote(buf.at[0], buf.at[1], near_s.at[i], near_r.at[i], ctx=c - 1)

    @pl.when(c + 2 < n)
    def _():
        for i in range(2):
            far(i).start()

    @pl.when(even)
    def _():
        for i in range(2):
            near(i).start()

    @pl.when(c < 2)
    def _():
        halo_k[0] = jnp.zeros((tok, width), jnp.bfloat16)
        halo_v[0] = jnp.zeros((tok, width), jnp.bfloat16)

    @pl.when(c < 1)
    def _():
        halo_k[1] = jnp.zeros((tok, width), jnp.bfloat16)
        halo_v[1] = jnp.zeros((tok, width), jnp.bfloat16)

    w_other = remote(
        ow.at[:, pl.ds(pl.multiple_of((1 - side) * cols, 128), cols)],
        wide.at[pl.ds(width, width)],
        w_s, w_r, head=1 - side,
    )
    w_own = pltpu.make_async_copy(
        ow.at[:, pl.ds(pl.multiple_of(side * cols, 128), cols)], wide.at[pl.ds(0, width)], w_l
    )
    w_other.start()
    w_own.start()

    def span(h):
        return slice(h * hs, (h + 1) * hs)

    token_ids = lax.broadcasted_iota(jnp.int32, (tok, 1), 0)
    valid = (token_ids < counts[c]).astype(jnp.float32)

    def wide_at(index):
        return pl.ds(pl.multiple_of(index * wide_rows, wide_rows), wide_rows)

    def row_at(layer_index):
        return pl.ds(pl.multiple_of(place * wide_rows + layer_index * rows, rows), rows)

    def plane_sum(h, d):
        return remote(
            grads.at[h, :, wide_at(lax.rem(place + d, plane))],
            part_in.at[h, d - 1],
            p1_s.at[h, d - 1], p1_r.at[h, d - 1], ctx=in_plane(d),
        )

    def line_sum(h, d):
        other = lax.rem(layer + d, depth)
        return remote(
            part.at[h, :, pl.ds(pl.multiple_of(other * rows, rows), rows)],
            last_in.at[h, d - 1],
            p2_s.at[h, d - 1], p2_r.at[h, d - 1], ctx=in_line(d),
        )

    def line_gather(h, d, source):
        held = fresh.at[h, :, row_at(source)]
        return remote(held, held, g1_s.at[h, d - 1], g1_r.at[h, d - 1], ctx=in_line(d))

    def plane_gather(h, d, source):
        held = fresh.at[h, :, wide_at(source)]
        return remote(held, held, g2_s.at[h, d - 1], g2_r.at[h, d - 1], ctx=in_plane(d))

    def line_source(d):
        return lax.rem(layer + depth - d, depth)

    def plane_source(d):
        return lax.rem(place + plane - d, plane)

    for h in range(heads):
        keys = k[:, span(h)]
        low = [fw[h, m].astype(jnp.bfloat16) for m in range(3)]
        gate_pre = dot(keys, low[0], NT)
        up_pre = dot(keys, low[1], NT)
        sig = jax.nn.sigmoid(gate_pre)
        gate_act = gate_pre * sig
        hidden = (gate_act * up_pre).astype(jnp.bfloat16)
        scaled = ((rates[:, h : h + 1] * valid) * v[:, span(h)].astype(jnp.float32)).astype(
            jnp.bfloat16
        )
        back = -dot(scaled, low[2], NN)
        grad_gate = (back * up_pre * (sig * (1.0 + gate_pre * (1.0 - sig)))).astype(jnp.bfloat16)
        grad_up = (back * gate_act).astype(jnp.bfloat16)
        grads[h, 0] = dot(grad_gate, keys, TN).astype(jnp.bfloat16)
        grads[h, 1] = dot(grad_up, keys, TN).astype(jnp.bfloat16)
        grads[h, 2] = (-dot(scaled, hidden, TN)).astype(jnp.bfloat16)
        for d in range(1, plane):
            plane_sum(h, d).start()

    for h in range(heads):
        total = grads[h, :, wide_at(place)].astype(jnp.float32)
        for d in range(1, plane):
            plane_sum(h, d).wait_recv()
            total += part_in[h, d - 1].astype(jnp.float32)
        part[h] = total.astype(jnp.bfloat16)
        for d in range(1, depth):
            line_sum(h, d).start()

    @pl.when(c >= 2)
    def _():
        for i in range(2):
            far(i).wait_recv()

            @pl.when(jnp.logical_not(even))
            def _():
                forward(i).start()

    for h in range(heads):
        total = part[h, :, pl.ds(pl.multiple_of(layer * rows, rows), rows)].astype(jnp.float32)
        for d in range(1, depth):
            line_sum(h, d).wait_recv()
            total += last_in[h, d - 1].astype(jnp.float32)
        fresh[h, :, row_at(layer)] = refresh(fw[h, :, row_at(layer)], total, tok * n)
        for d in range(1, depth):
            line_gather(h, d, layer).start()

    for h in range(heads):
        for d in range(1, depth):
            line_gather(h, d, line_source(d)).wait_recv()
        for d in range(1, plane):
            plane_gather(h, d, place).start()

    @pl.when(c >= 1)
    def _():
        for i in range(2):
            near(i).wait_recv()

    key_ids = lax.broadcasted_iota(jnp.int32, (tok, tok), 1)
    row_ids = lax.broadcasted_iota(jnp.int32, (tok, tok), 0)
    count_2 = jnp.where(c >= 2, counts[jnp.maximum(c - 2, 0)], 0)
    count_1 = jnp.where(c >= 1, counts[jnp.maximum(c - 1, 0)], 0)
    allowed = (
        (key_ids > row_ids) & (key_ids < count_2),
        key_ids < count_1,
        (key_ids <= row_ids) & (key_ids < counts[c]),
    )
    for h in range(heads):
        asked = q[:, span(h)]
        scores = [
            jnp.where(ok, dot(asked, held, NT) / math.sqrt(hs), -1e30)
            for ok, held in zip(
                allowed, (halo_k[0, :, span(h)], halo_k[1, :, span(h)], k[:, span(h)])
            )
        ]
        top = functools.reduce(
            jnp.maximum, [jnp.max(s, axis=-1, keepdims=True) for s in scores]
        )
        expo = [jnp.exp(s - top) for s in scores]
        norm = sum(jnp.sum(e, axis=-1, keepdims=True) for e in expo)
        window[:, span(h)] = sum(
            dot((e / norm).astype(jnp.bfloat16), held, NN)
            for e, held in zip(
                expo, (halo_v[0, :, span(h)], halo_v[1, :, span(h)], v[:, span(h)])
            )
        )

    def feature_swap(h):
        return remote(
            feats.at[:, span(h)],
            feats.at[:, slice(width + h * hs, width + (h + 1) * hs)],
            f_s.at[h], f_r.at[h], head=1 - side,
        )

    for h in range(heads):
        for d in range(1, plane):
            plane_gather(h, d, plane_source(d)).wait_recv()
        asked = q[:, span(h)]
        query_gate = dot(asked, fresh[h, 0], NT)
        query_up = dot(asked, fresh[h, 1], NT)
        query_hidden = (query_gate * jax.nn.sigmoid(query_gate) * query_up).astype(jnp.bfloat16)
        ttt_out = dot(query_hidden, fresh[h, 2], NT)
        feats[:, span(h)] = ((ttt_out + window[:, span(h)]) * valid).astype(jnp.bfloat16)
        feature_swap(h).start()

    w_own.wait()
    w_other.wait_recv()
    for h in range(heads):
        feature_swap(h).wait_recv()
    all_features = feats[...]
    step = min(cols, 512)
    for at in range(0, cols, step):
        out[:, at : at + step] = dot(all_features, wide[:, at : at + step], NN).astype(out.dtype)

    w_other.wait_send()
    for h in range(heads):
        feature_swap(h).wait_send()
        for d in range(1, plane):
            plane_sum(h, d).wait_send()
            plane_gather(h, d, place).wait_send()
        for d in range(1, depth):
            line_sum(h, d).wait_send()
            line_gather(h, d, layer).wait_send()

    @pl.when(c + 2 < n)
    def _():
        for i in range(2):
            far(i).wait_send()

    @pl.when(even)
    def _():
        for i in range(2):
            near(i).wait_send()

    @pl.when(jnp.logical_not(even) & (c >= 2))
    def _():
        for i in range(2):
            forward(i).wait_send()


def shards(queries, token_keys, token_values, step_rates, counts, fast_weights, out_weight, *, n, plane):
    tok, heads, hs = queries.shape
    width = heads * hs
    depth = n // plane
    cols = out_weight.shape[1] // 2
    vmem, dma = pltpu.VMEM, pltpu.SemaphoreType.DMA
    bf16, f32 = jnp.bfloat16, jnp.float32
    wide_rows, rows = hs // plane, hs // n
    in_vmem = pl.BlockSpec(memory_space=pltpu.VMEM)
    return pl.pallas_call(
        functools.partial(kernel, n, plane),
        out_shape=jax.ShapeDtypeStruct((tok, cols), bf16),
        in_specs=[pl.BlockSpec(memory_space=pltpu.SMEM)]
        + [in_vmem] * 5
        + [pl.BlockSpec(memory_space=pltpu.HBM)],
        out_specs=in_vmem,
        scratch_shapes=[
            vmem((heads, 3, hs, hs), bf16),
            vmem((heads, plane - 1, 3, wide_rows, hs), bf16),
            vmem((heads, 3, wide_rows, hs), bf16),
            vmem((heads, depth - 1, 3, rows, hs), bf16),
            vmem((heads, 3, hs, hs), bf16),
            vmem((2, tok, width), bf16),
            vmem((2, tok, width), bf16),
            vmem((tok, width), f32),
            vmem((2 * width, cols), bf16),
            vmem((tok, 2 * width), bf16),
            dma((heads, plane - 1)), dma((heads, plane - 1)),
            dma((heads, depth - 1)), dma((heads, depth - 1)),
            dma((heads, depth - 1)), dma((heads, depth - 1)),
            dma((heads, plane - 1)), dma((heads, plane - 1)),
            dma((2,)), dma((2,)), dma((2,)), dma((2,)),
            dma, dma, dma,
            dma((heads,)), dma((heads,)),
        ],
        compiler_params=pltpu.CompilerParams(
            collective_id=0, has_side_effects=True, vmem_limit_bytes=48 * 1024 * 1024
        ),
        name="layer",
    )(
        counts,
        queries.reshape(tok, width),
        token_keys.reshape(tok, width),
        token_values.reshape(tok, width),
        step_rates,
        fast_weights,
        out_weight,
    )


def fitting_plane(n, hs):
    if n % 2 or hs % (16 * n):
        return 0
    plane = max(p for p in range(1, math.isqrt(n) + 1) if n % p == 0)
    return plane if plane > 1 else 0


def solution(mesh):
    in_specs = (
        P("ctx", "head", None),
        P("ctx", "head", None),
        P("ctx", "head", None),
        P("ctx", "head"),
        P(),
        P("head", None, None, None),
        P("head", None),
    )
    out_specs = P("ctx", "head")
    n = mesh.shape["ctx"]

    def layer(*args):
        hs = args[5].shape[-1]
        plane = fitting_plane(n, hs) if mesh.shape["head"] == 2 else 0
        body = functools.partial(shards, n=n, plane=plane) if plane else plain_shards
        return jax.shard_map(
            body, mesh=mesh, in_specs=in_specs, out_specs=out_specs, check_vma=False
        )(*args)

    return layer
```

```python
import functools
import math

import jax
import jax.numpy as jnp
from jax import lax
from jax.experimental import pallas as pl
from jax.experimental.pallas import tpu as pltpu
from jax.sharding import PartitionSpec as P

SPAN = 2
FIRST_AT = {"entry": (0, 1), "lined 0": (2,), "lined 1": (3,)}
SECOND_AT = {"summed 0": (0,), "summed 1": (1,), "fresh 0": (2,), "fresh 1": (3,)}
NT = (((1,), (1,)), ((), ()))
NN = (((1,), (0,)), ((), ()))
TN = (((0,), (0,)), ((), ()))


def dot(a, b, dims):
    return lax.dot_general(a, b, dims, preferred_element_type=jnp.float32)


def passed_along(value, axis, steps):
    count = lax.axis_size(axis)
    leading, last = (max(0, -steps), min(count, count - steps))
    return lax.ppermute(value, axis, [(source, source + steps) for source in range(leading, last)])


def silu_slope(pre_value):
    sigmoid_value = jax.nn.sigmoid(pre_value)
    return sigmoid_value * (1.0 + pre_value * (1.0 - sigmoid_value))


def refresh(old_rows, gradient_rows, token_total):
    updated = old_rows - gradient_rows / math.sqrt(token_total)
    old_norm = jnp.sqrt(jnp.sum(old_rows * old_rows, axis=-1, keepdims=True))
    fresh = (
        updated * old_norm / jnp.sqrt(jnp.sum(updated * updated, axis=-1, keepdims=True) + 1e-06)
    )
    return fresh.astype(jnp.bfloat16)


def plain_shards(queries, token_keys, token_values, step_rates, counts, fast_weights, out_weight):
    tok_rows, head_local, head_width = queries.shape
    device_count = lax.axis_size("ctx")
    device_place = lax.axis_index("ctx")
    positions = jnp.arange(tok_rows, dtype=jnp.int32)
    own_count = lax.dynamic_index_in_dim(counts, device_place, 0, keepdims=False)
    valid_rows = (positions < own_count).astype(jnp.float32)
    weights_low = fast_weights.astype(jnp.bfloat16)
    gate_pre = jnp.einsum(
        "thi,hci->thc", token_keys, weights_low[:, 0], preferred_element_type=jnp.float32
    )
    up_pre = jnp.einsum(
        "thi,hci->thc", token_keys, weights_low[:, 1], preferred_element_type=jnp.float32
    )
    gate_act = jax.nn.silu(gate_pre)
    hidden = (gate_act * up_pre).astype(jnp.bfloat16)
    scaled = (
        (step_rates * valid_rows[:, None])[:, :, None] * token_values.astype(jnp.float32)
    ).astype(jnp.bfloat16)
    grad_down = -jnp.einsum("thd,thc->hdc", scaled, hidden, preferred_element_type=jnp.float32)
    back_hidden = -jnp.einsum(
        "thd,hdc->thc", scaled, weights_low[:, 2], preferred_element_type=jnp.float32
    )
    grad_gate = (back_hidden * up_pre * silu_slope(gate_pre)).astype(jnp.bfloat16)
    grad_up = (back_hidden * gate_act).astype(jnp.bfloat16)
    first_grad = jnp.einsum(
        "thc,thi->hci", grad_gate, token_keys, preferred_element_type=jnp.float32
    )
    second_grad = jnp.einsum(
        "thc,thi->hci", grad_up, token_keys, preferred_element_type=jnp.float32
    )
    local_grad = jnp.stack([first_grad, second_grad, grad_down], axis=1).reshape(-1, head_width)
    old_flat = fast_weights.reshape(-1, head_width)
    token_total = tok_rows * device_count
    grad_whole = lax.psum(local_grad, "ctx")
    new_flat = refresh(old_flat, grad_whole, token_total)
    new_weights = new_flat.reshape(head_local, 3, head_width, head_width)
    query_gate = jnp.einsum(
        "thi,hci->thc", queries, new_weights[:, 0], preferred_element_type=jnp.float32
    )
    query_up = jnp.einsum(
        "thi,hci->thc", queries, new_weights[:, 1], preferred_element_type=jnp.float32
    )
    query_hidden = (jax.nn.silu(query_gate) * query_up).astype(jnp.bfloat16)
    ttt_out = jnp.einsum(
        "thc,hdc->thd", query_hidden, new_weights[:, 2], preferred_element_type=jnp.float32
    )
    key_parts = []
    value_parts = []
    valid_parts = []
    for back_step in range(SPAN, 0, -1):
        moved_keys, moved_values = passed_along((token_keys, token_values), "ctx", back_step)
        source = device_place - back_step
        source_count = lax.dynamic_index_in_dim(counts, jnp.maximum(source, 0), 0, keepdims=False)
        valid_parts.append(((positions < source_count) & (source >= 0)).astype(jnp.float32))
        key_parts.append(moved_keys)
        value_parts.append(moved_values)
    key_parts.append(token_keys)
    value_parts.append(token_values)
    valid_parts.append(valid_rows)
    seen_keys = jnp.concatenate(key_parts, 0)
    seen_values = jnp.concatenate(value_parts, 0)
    seen_valid = jnp.concatenate(valid_parts, 0)
    window_len = SPAN * tok_rows
    distance = (
        window_len
        + positions[:, None]
        - jnp.arange(window_len + tok_rows, dtype=jnp.int32)[None, :]
    )
    scores = jnp.einsum(
        "thi,shi->hts", queries, seen_keys, preferred_element_type=jnp.float32
    ) / math.sqrt(head_width)
    allowed = (distance >= 0) & (distance < window_len) & (seen_valid[None, :] > 0.5)
    scores = jnp.where(allowed[None], scores, -1e30)
    top_score = jnp.max(scores, axis=-1, keepdims=True)
    expo = jnp.exp(scores - top_score)
    attention = (expo / jnp.sum(expo, axis=-1, keepdims=True)).astype(jnp.bfloat16)
    window_out = jnp.einsum(
        "hts,shd->thd", attention, seen_values, preferred_element_type=jnp.float32
    )
    features = ((ttt_out + window_out) * valid_rows[:, None, None]).astype(jnp.bfloat16)
    features = features.reshape(tok_rows, head_local * head_width)
    partial_out = jnp.dot(features, out_weight, preferred_element_type=jnp.float32)
    return lax.psum_scatter(
        partial_out.astype(jnp.bfloat16), "head", scatter_dimension=1, tiled=True
    )


def kernel(
    n, plane, counts_in, q_in, k_in, v_in, rates_in, fw_in, ow, out,
    counts, q, k, v, rates, fw, in_s, grads, part_in, part, last_in, fresh, halo_k, halo_v, window, wide, feats,
    p1_s, p1_r, p2_s, p2_r, g1_s, g1_r, g2_s, g2_r, far_s, far_r, near_s, near_r,
    w_s, w_r, w_l, f_s, f_r,
):
    tok, heads, hs = k.shape
    width = heads * hs
    depth = n // plane
    wide_rows, rows = hs // plane, hs // n
    cols = out.shape[1]
    c, side = lax.axis_index("ctx"), lax.axis_index("head")
    place, layer = lax.rem(c, plane), lax.div(c, plane)
    even = lax.rem(c, 2) == 0

    def in_plane(d):
        return layer * plane + lax.rem(place + d, plane)

    def in_line(d):
        return lax.rem(layer + d, depth) * plane + place

    def remote(src, dst, send, recv, **device):
        return pltpu.make_async_remote_copy(
            src, dst, send, recv, device_id=device, device_id_type=pl.DeviceIdType.MESH
        )

    fetch_counts = pltpu.make_async_copy(counts_in, counts, in_s.at[0])
    fetch_rates = pltpu.make_async_copy(rates_in, rates, in_s.at[1])
    fetch_q = pltpu.make_async_copy(q_in, q, in_s.at[2])
    fetch_fw = [
        pltpu.make_async_copy(fw_in.at[h], fw.at[h], in_s.at[3 + h]) for h in range(heads)
    ]
    fetch_k = pltpu.make_async_copy(k_in, k, in_s.at[3 + heads])
    fetch_v = pltpu.make_async_copy(v_in, v, in_s.at[4 + heads])
    for copy in (fetch_k, fetch_v, *fetch_fw, fetch_counts, fetch_rates, fetch_q):
        copy.start()

    barrier = pltpu.get_barrier_semaphore()

    def greet(**device):
        pl.semaphore_signal(
            barrier, inc=1, device_id=device, device_id_type=pl.DeviceIdType.MESH
        )

    for d in range(1, plane):
        greet(ctx=in_plane(d))
    for d in range(1, depth):
        greet(ctx=in_line(d))
    greet(head=1 - side)

    @pl.when(c >= 2)
    def _():
        greet(ctx=c - 2)

    @pl.when(jnp.logical_not(even))
    def _():
        greet(ctx=c - 1)

    @pl.when(even & (c >= 2))
    def _():
        greet(ctx=c + 1)

    sends = (
        plane + depth - 1
        + jnp.where(c + 2 < n, 1, 0)
        + jnp.where(even | (c >= 2), 1, 0)
    )
    pl.semaphore_wait(barrier, sends)

    half = tok // 2

    def piece(i):
        at = pl.ds((i // 2) * half, half)
        return ((k_in, halo_k), (v_in, halo_v))[i % 2] + (at,)

    def far(i):
        src, dst, at = piece(i)
        return remote(src.at[at], dst.at[0, at], far_s.at[i], far_r.at[i], ctx=c + 2)

    def near(i):
        src, dst, at = piece(i)
        return remote(src.at[at], dst.at[1, at], near_s.at[i], near_r.at[i], ctx=c + 1)

    def forward(i):
        _, buf, at = piece(i)
        return remote(buf.at[0, at], buf.at[1, at], near_s.at[i], near_r.at[i], ctx=c - 1)

    def send_halo(point):
        firsts, seconds = FIRST_AT.get(point, ()), SECOND_AT.get(point, ())
        if firsts:
            @pl.when(c + 2 < n)
            def _():
                for i in firsts:
                    far(i).start()

            @pl.when(even)
            def _():
                for i in firsts:
                    near(i).start()

        if seconds:
            @pl.when(jnp.logical_not(even) & (c >= 2))
            def _():
                for i in seconds:
                    far(i).wait_recv()
                    forward(i).start()

    send_halo("entry")

    @pl.when(c < 2)
    def _():
        halo_k[0] = jnp.zeros((tok, heads, hs), jnp.bfloat16)
        halo_v[0] = jnp.zeros((tok, heads, hs), jnp.bfloat16)

    @pl.when(c < 1)
    def _():
        halo_k[1] = jnp.zeros((tok, heads, hs), jnp.bfloat16)
        halo_v[1] = jnp.zeros((tok, heads, hs), jnp.bfloat16)

    w_other = remote(
        ow.at[:, pl.ds(pl.multiple_of((1 - side) * cols, 128), cols)],
        wide.at[pl.ds(width, width)],
        w_s, w_r, head=1 - side,
    )
    w_own = pltpu.make_async_copy(
        ow.at[:, pl.ds(pl.multiple_of(side * cols, 128), cols)], wide.at[pl.ds(0, width)], w_l
    )
    w_other.start()
    w_own.start()

    def span(h):
        return slice(h * hs, (h + 1) * hs)

    fetch_counts.wait()
    fetch_rates.wait()
    fetch_k.wait()
    fetch_v.wait()
    token_ids = lax.broadcasted_iota(jnp.int32, (tok, 1), 0)
    valid = (token_ids < counts[c]).astype(jnp.float32)

    def wide_at(index):
        return pl.ds(pl.multiple_of(index * wide_rows, wide_rows), wide_rows)

    def row_at(layer_index):
        return pl.ds(pl.multiple_of(place * wide_rows + layer_index * rows, rows), rows)

    def plane_sum(h, d):
        return remote(
            grads.at[h, :, wide_at(lax.rem(place + d, plane))],
            part_in.at[h, d - 1],
            p1_s.at[h, d - 1], p1_r.at[h, d - 1], ctx=in_plane(d),
        )

    def line_sum(h, d):
        other = lax.rem(layer + d, depth)
        return remote(
            part.at[h, :, pl.ds(pl.multiple_of(other * rows, rows), rows)],
            last_in.at[h, d - 1],
            p2_s.at[h, d - 1], p2_r.at[h, d - 1], ctx=in_line(d),
        )

    def line_gather(h, d, source):
        held = fresh.at[h, :, row_at(source)]
        return remote(held, held, g1_s.at[h, d - 1], g1_r.at[h, d - 1], ctx=in_line(d))

    def plane_gather(h, d, source):
        held = fresh.at[h, :, wide_at(source)]
        return remote(held, held, g2_s.at[h, d - 1], g2_r.at[h, d - 1], ctx=in_plane(d))

    def line_source(d):
        return lax.rem(layer + depth - d, depth)

    def plane_source(d):
        return lax.rem(place + plane - d, plane)

    for h in range(heads):
        fetch_fw[h].wait()
        keys = k[:, h, :]
        rate = jnp.broadcast_to(rates[h : h + 1, :], (8, tok)).T[:, 0:1]
        low = [fw[h, m].astype(jnp.bfloat16) for m in range(3)]
        gate_pre = dot(keys, low[0], NT)
        up_pre = dot(keys, low[1], NT)
        sig = jax.nn.sigmoid(gate_pre)
        gate_act = gate_pre * sig
        hidden = (gate_act * up_pre).astype(jnp.bfloat16)
        scaled = ((rate * valid) * v[:, h, :].astype(jnp.float32)).astype(
            jnp.bfloat16
        )
        back = -dot(scaled, low[2], NN)
        grad_gate = (back * up_pre * (sig * (1.0 + gate_pre * (1.0 - sig)))).astype(jnp.bfloat16)
        grad_up = (back * gate_act).astype(jnp.bfloat16)
        grads[h, 0] = dot(grad_gate, keys, TN).astype(jnp.bfloat16)
        grads[h, 1] = dot(grad_up, keys, TN).astype(jnp.bfloat16)
        grads[h, 2] = (-dot(scaled, hidden, TN)).astype(jnp.bfloat16)
        for d in range(1, plane):
            plane_sum(h, d).start()
        send_halo(f"summed {h}")

    for h in range(heads):
        total = grads[h, :, wide_at(place)].astype(jnp.float32)
        for d in range(1, plane):
            plane_sum(h, d).wait_recv()
            total += part_in[h, d - 1].astype(jnp.float32)
        part[h] = total.astype(jnp.bfloat16)
        for d in range(1, depth):
            line_sum(h, d).start()
        send_halo(f"lined {h}")

    for h in range(heads):
        total = part[h, :, pl.ds(pl.multiple_of(layer * rows, rows), rows)].astype(jnp.float32)
        for d in range(1, depth):
            line_sum(h, d).wait_recv()
            total += last_in[h, d - 1].astype(jnp.float32)
        fresh[h, :, row_at(layer)] = refresh(fw[h, :, row_at(layer)], total, tok * n)
        for d in range(1, depth):
            line_gather(h, d, layer).start()
        send_halo(f"fresh {h}")

    for h in range(heads):
        for d in range(1, depth):
            line_gather(h, d, line_source(d)).wait_recv()
        for d in range(1, plane):
            plane_gather(h, d, place).start()
        send_halo(f"gathered {h}")

    fetch_q.wait()

    @pl.when(even & (c >= 2))
    def _():
        for i in range(4):
            far(i).wait_recv()

    @pl.when(c >= 1)
    def _():
        for i in range(4):
            near(i).wait_recv()

    key_ids = lax.broadcasted_iota(jnp.int32, (tok, tok), 1)
    row_ids = lax.broadcasted_iota(jnp.int32, (tok, tok), 0)
    count_2 = jnp.where(c >= 2, counts[jnp.maximum(c - 2, 0)], 0)
    count_1 = jnp.where(c >= 1, counts[jnp.maximum(c - 1, 0)], 0)
    allowed = (
        (key_ids > row_ids) & (key_ids < count_2),
        key_ids < count_1,
        (key_ids <= row_ids) & (key_ids < counts[c]),
    )
    for h in range(heads):
        asked = q[:, h, :]
        scores = [
            jnp.where(ok, dot(asked, held, NT) / math.sqrt(hs), -1e30)
            for ok, held in zip(
                allowed, (halo_k[0, :, h, :], halo_k[1, :, h, :], k[:, h, :])
            )
        ]
        top = functools.reduce(
            jnp.maximum, [jnp.max(s, axis=-1, keepdims=True) for s in scores]
        )
        expo = [jnp.exp(s - top) for s in scores]
        norm = sum(jnp.sum(e, axis=-1, keepdims=True) for e in expo)
        window[:, span(h)] = sum(
            dot((e / norm).astype(jnp.bfloat16), held, NN)
            for e, held in zip(
                expo, (halo_v[0, :, h, :], halo_v[1, :, h, :], v[:, h, :])
            )
        )

    def feature_swap(h):
        return remote(
            feats.at[:, span(h)],
            feats.at[:, slice(width + h * hs, width + (h + 1) * hs)],
            f_s.at[h], f_r.at[h], head=1 - side,
        )

    for h in range(heads):
        for d in range(1, plane):
            plane_gather(h, d, plane_source(d)).wait_recv()
        asked = q[:, h, :]
        query_gate = dot(asked, fresh[h, 0], NT)
        query_up = dot(asked, fresh[h, 1], NT)
        query_hidden = (query_gate * jax.nn.sigmoid(query_gate) * query_up).astype(jnp.bfloat16)
        ttt_out = dot(query_hidden, fresh[h, 2], NT)
        feats[:, span(h)] = ((ttt_out + window[:, span(h)]) * valid).astype(jnp.bfloat16)
        feature_swap(h).start()

    w_own.wait()
    w_other.wait_recv()
    for h in range(heads):
        feature_swap(h).wait_recv()
    all_features = feats[...]
    step = min(cols, 512)
    for at in range(0, cols, step):
        out[:, at : at + step] = dot(all_features, wide[:, at : at + step], NN).astype(out.dtype)

    w_other.wait_send()
    for h in range(heads):
        feature_swap(h).wait_send()
        for d in range(1, plane):
            plane_sum(h, d).wait_send()
            plane_gather(h, d, place).wait_send()
        for d in range(1, depth):
            line_sum(h, d).wait_send()
            line_gather(h, d, layer).wait_send()

    @pl.when(c + 2 < n)
    def _():
        for i in range(4):
            far(i).wait_send()

    @pl.when(even)
    def _():
        for i in range(4):
            near(i).wait_send()

    @pl.when(jnp.logical_not(even) & (c >= 2))
    def _():
        for i in range(4):
            forward(i).wait_send()


def shards(queries, token_keys, token_values, step_rates, counts, fast_weights, out_weight, *, n, plane):
    tok, heads, hs = queries.shape
    width = heads * hs
    depth = n // plane
    cols = out_weight.shape[1] // 2
    vmem, dma = pltpu.VMEM, pltpu.SemaphoreType.DMA
    bf16, f32 = jnp.bfloat16, jnp.float32
    wide_rows, rows = hs // plane, hs // n
    in_hbm = pl.BlockSpec(memory_space=pltpu.HBM)
    in_vmem = pl.BlockSpec(memory_space=pltpu.VMEM)
    return pl.pallas_call(
        functools.partial(kernel, n, plane),
        out_shape=jax.ShapeDtypeStruct((tok, cols), bf16),
        in_specs=[in_hbm] * 7,
        out_specs=in_vmem,
        scratch_shapes=[
            pltpu.SMEM(counts.shape, jnp.int32),
            vmem(queries.shape, bf16),
            vmem(queries.shape, bf16),
            vmem(queries.shape, bf16),
            vmem((heads, tok), f32),
            vmem(fast_weights.shape, f32),
            dma((5 + heads,)),
            vmem((heads, 3, hs, hs), bf16),
            vmem((heads, plane - 1, 3, wide_rows, hs), bf16),
            vmem((heads, 3, wide_rows, hs), bf16),
            vmem((heads, depth - 1, 3, rows, hs), bf16),
            vmem((heads, 3, hs, hs), bf16),
            vmem((2, tok, heads, hs), bf16),
            vmem((2, tok, heads, hs), bf16),
            vmem((tok, width), f32),
            vmem((2 * width, cols), bf16),
            vmem((tok, 2 * width), bf16),
            dma((heads, plane - 1)), dma((heads, plane - 1)),
            dma((heads, depth - 1)), dma((heads, depth - 1)),
            dma((heads, depth - 1)), dma((heads, depth - 1)),
            dma((heads, plane - 1)), dma((heads, plane - 1)),
            dma((4,)), dma((4,)), dma((4,)), dma((4,)),
            dma, dma, dma,
            dma((heads,)), dma((heads,)),
        ],
        compiler_params=pltpu.CompilerParams(
            collective_id=0, has_side_effects=True, vmem_limit_bytes=60 * 1024 * 1024
        ),
        name="layer",
    )(
        counts,
        queries,
        token_keys,
        token_values,
        step_rates.T,
        fast_weights,
        out_weight,
    )


def fitting_plane(n, hs):
    if n % 2 or hs % (16 * n):
        return 0
    plane = max(p for p in range(1, math.isqrt(n) + 1) if n % p == 0)
    return plane if plane > 1 else 0


def solution(mesh):
    in_specs = (
        P("ctx", "head", None),
        P("ctx", "head", None),
        P("ctx", "head", None),
        P("ctx", "head"),
        P(),
        P("head", None, None, None),
        P("head", None),
    )
    out_specs = P("ctx", "head")
    n = mesh.shape["ctx"]

    def layer(*args):
        hs = args[5].shape[-1]
        plane = fitting_plane(n, hs) if mesh.shape["head"] == 2 else 0
        body = functools.partial(shards, n=n, plane=plane) if plane else plain_shards
        return jax.shard_map(
            body, mesh=mesh, in_specs=in_specs, out_specs=out_specs, check_vma=False
        )(*args)

    return layer
```
